128 devices in a mesh: expert: 64 (over z, x, y_hi, core), dp: 2 (over y_lo).
Axes of the slice: x: 4, y: 4 (y_hi: 2, y_lo: 2; y = y_hi * 2 + y_lo), z: 4, core: 2. Of those that a mesh axis runs over, the one named last changes fastest.
Arguments:
- tokens: bfloat16 [4, 2048, 2048], P(None, ('dp', 'expert')), parts along dimension 1, may hold values from -6 to 6
- routes: int32 [4, 2048, 8], P(None, ('dp', 'expert')), parts along dimension 1, may hold values from 0 to 63, all different within a row; in each aligned block of 16 rows (0 to 15, 16 to 31, ..., all dimensions but the last counted through in order) at most 4 rows name the same one
- route_gates: float32 [4, 2048, 8], P(None, ('dp', 'expert')), parts along dimension 1, may hold values from 0.05 to 1
- w_gate_up: bfloat16 [64, 2048, 1536], P('expert'), may hold values from -0.125 to 0.125
- w_down: bfloat16 [64, 768, 2048], P('expert'), may hold values from -0.21875 to 0.21875
- owner_before: int32 [64], replicated, may hold values from 0 to 63, each once
- swap_flags: int32 [64], replicated, may hold values from 0 to 1, as said below
Outputs:
- mixed_tokens: bfloat16 [4, 2048, 2048], P(None, ('dp', 'expert')), parts along dimension 1
- load: float32 [128], P(('dp', 'expert')), parts along dimension 0
- held_gate_up: bfloat16 [128, 2048, 1536], P(('dp', 'expert')), parts along dimension 0
- held_down: bfloat16 [128, 768, 2048], P(('dp', 'expert')), parts along dimension 0
The draws below stay inside these ranges and needn't reach their ends.
There are 2 independent parts, one for each index of `dp`. The reference program is written for one: setup_inputs(seed, part) draws one part's arguments, and reference() takes and returns one part's arrays. A program takes and returns all parts, laid end to end along the dimension named above; an argument that names none is the same for every part. Nothing has to cross between parts.
Inputs may be any that keep to these rules, and one draw needn't show every extreme that they name: `routes`: within the tokens of one device in one micro-batch (aligned blocks of 16 rows of a micro-batch), no expert is named more than 4 times, a bound that some block reaches. `owner_before`: each device holds exactly one expert. swap_flags[i] equals swap_flags[i + 32] for i < 32.
All inputs are finite; a program needn't handle non-finite values.
Results may differ from the reference program's by a relative error of at most 0.0058.
Values may be sent and summed in bfloat16 or wider, within the bound.
A program may use at most 128 MiB of HBM per device.

```python
import math
import jax
import jax.numpy as jnp
import numpy as np
from jax import lax

D = 2048
FFW = 768
TOP = 8
MB = 4
MB_TOK = 16
EXPERTS = 64
TOKENS = 1024
CAP = 4


def draw_swap_flags(key, part):
    flags = jax.random.randint(key, (EXPERTS // 2,), 0, 2).astype(jnp.int32)
    return jnp.concatenate([flags, flags])


def block_levels(rng, extent, cuts, least, top_value):
    gain, own = 1.0, jax.random.fold_in(rng, 6)
    for position, shards_of in cuts:
        heights = jnp.exp(jax.random.uniform(jax.random.fold_in(own, position), (shards_of,), jnp.float32, least / len(cuts), top_value / len(cuts)))
        gain = gain * jnp.repeat(heights, extent[position] // shards_of).reshape([-1 if axis == position else 1 for axis in range(len(extent))])
    return gain


def deal_out(stream_key, own, number, rows, number_of, top, bound, slope):
    order = jax.random.permutation(stream_key, number_of)
    heavy_load, common = shares(number_of, rows * top, bound, slope, True), shares(number_of, rows * top, bound, slope, False)
    places = jnp.arange(number_of)

    def named(tallies, offset_by):
        used = int((tallies > 0).sum())
        fixed = max(1, used // 4)
        shifted = fixed + (places - fixed + offset_by * (used - fixed)) % max(1, number_of - fixed)
        return jnp.zeros((number_of,), jnp.int32).at[order[jnp.where(places < fixed, places, shifted)]].set(jnp.asarray(tallies, jnp.int32))

    tallies = jnp.where(number % 4 == 0, named(heavy_load, number // 4), named(common, number - number // 4 - 1))
    mixed = jax.random.permutation(jax.random.fold_in(own, 3), number_of)
    donor, receiver = mixed[0:number_of // 2 * 2:2], mixed[1:number_of // 2 * 2:2]
    slack = jnp.minimum(tallies[donor] - 1, bound - tallies[receiver]) // 2
    slack = jnp.where((donor == order[0]) | (receiver == order[0]) | (tallies[receiver] == 0), 0, jnp.maximum(slack, 0))
    shifted = jax.random.randint(jax.random.fold_in(own, 4), (number_of // 2,), 0, 1 << 20) % (slack + 1)
    tallies = tallies.at[donor].add(-shifted).at[receiver].add(shifted)
    items = jnp.searchsorted(jnp.cumsum(tallies), jnp.arange(rows * top), side="right").astype(jnp.int32)
    grid = items.reshape(top, rows).T
    grid = grid[jax.random.permutation(jax.random.fold_in(own, 1), rows)]
    offset_by = jax.random.randint(jax.random.fold_in(own, 2), (rows, 1), 0, top)
    return jnp.take_along_axis(grid, (jnp.arange(top)[None, :] + offset_by) % top, axis=1)


def shares(number_of, total, reach, skew, full):
    weights = [(1 << 20) // math.isqrt(standing ** skew) + 1 for standing in range(1, number_of + 1)]
    largest = reach if full else min(reach, max(-(-total // number_of), total * weights[0] // sum(weights)))
    least = 1 if total - largest >= number_of - 1 else 0
    counts, spare = [largest] + [least] * (number_of - 1), total - largest - least * (number_of - 1)
    while spare > 0:
        free = [i for i in range(1, number_of) if counts[i] < largest] or [i for i in range(1, number_of) if counts[i] < reach]
        whole, left = sum([weights[i] for i in free]), spare
        for i in free:
            extra = min(reach - counts[i], max(1, left * weights[i] // whole), spare)
            counts[i] = counts[i] + extra
            spare = spare - extra
    return np.array(counts)


def centred(own_key, dims, scale, most, shards=(), held_as=jnp.bfloat16):
    level = block_levels(own_key, dims, shards, -0.22, 0.18) if shards else 1.0
    drawn = jax.random.normal(own_key, dims, jnp.float32) * scale * level
    return jnp.minimum(jnp.maximum(drawn, -most), most).astype(held_as)


def setup_inputs(seed: int = 0, part: int = 0) -> dict:
    arg_keys = jax.random.split(jax.random.key(seed), 8)
    own_keys = jax.random.split(jax.random.fold_in(arg_keys[7], part), 8)
    tokens = centred(own_keys[0], (MB, TOKENS, D), 1.0, 6.0, ((1, 64),))
    routes_keys = jax.random.split(jax.random.fold_in(own_keys[1], 1), MB * TOKENS // MB_TOK)
    routes_turns = jax.random.permutation(jax.random.fold_in(own_keys[1], 3), MB * TOKENS // MB_TOK)
    routes = jax.vmap(lambda own, number: deal_out(jax.random.fold_in(own_keys[1], 2), own, number, MB_TOK, EXPERTS, TOP, CAP, 2))(routes_keys, routes_turns).reshape((MB, TOKENS, TOP))
    route_gates = jnp.clip(jnp.exp(math.log(1.0) - 2.9957323 * jax.random.uniform(own_keys[2], (MB, TOKENS, TOP), jnp.float32) ** block_levels(own_keys[2], (MB, TOKENS, TOP), ((1, 64),), -0.2, 0.2)), 0.05, 1.0)
    w_gate_up = centred(arg_keys[3], (EXPERTS, D, 2 * FFW), D ** -0.5, 0.125, ((0, 64),))
    w_down = centred(arg_keys[4], (EXPERTS, FFW, D), FFW ** -0.5, 0.21875, ((0, 64),))
    owner_before = jax.random.permutation(arg_keys[5], EXPERTS).astype(jnp.int32)
    swap_flags = draw_swap_flags(jax.random.fold_in(arg_keys[7], 71), part)
    return dict(tokens=tokens, routes=routes, route_gates=route_gates, w_gate_up=w_gate_up, w_down=w_down, owner_before=owner_before, swap_flags=swap_flags)


def ranking_of(flattened):
    onehot = (flattened[:, None] == jnp.arange(EXPERTS, dtype=jnp.int32)[None, :]).astype(jnp.int32)
    return jnp.sum((jnp.cumsum(onehot, axis=0) - 1) * onehot, axis=1).astype(jnp.int32)


def expert_ffn(inputs, gate_up, down_weight):
    hidden = jnp.dot(inputs.astype(jnp.float32), gate_up.astype(jnp.float32), precision=lax.Precision.HIGHEST)
    activated = (jax.nn.silu(hidden[:, :FFW]) * hidden[:, FFW:]).astype(jnp.bfloat16)
    return jnp.dot(activated.astype(jnp.float32), down_weight.astype(jnp.float32), precision=lax.Precision.HIGHEST).astype(jnp.bfloat16)


def reference(tokens, routes, route_gates, w_gate_up, w_down, owner_before, swap_flags):
    halfway = EXPERTS // 2
    swapped = swap_flags[owner_before] == 1
    owner_after = jnp.where(swapped, jnp.bitwise_xor(owner_before, halfway), owner_before).astype(jnp.int32)
    sources = jnp.broadcast_to(jnp.arange(EXPERTS, dtype=jnp.int32)[:, None], (EXPERTS, MB_TOK * TOP))
    token_ids = (sources * MB_TOK + (jnp.arange(MB_TOK * TOP, dtype=jnp.int32) // TOP)[None, :]).astype(jnp.int32)

    def serve(operands):
        inputs, holder = operands
        gate_up = lax.dynamic_index_in_dim(w_gate_up, holder, 0, keepdims=False)
        down_weight = lax.dynamic_index_in_dim(w_down, holder, 0, keepdims=False)
        return expert_ffn(inputs, gate_up, down_weight)

    outputs = []
    for batch_index in range(MB):
        blocks = routes[batch_index].reshape(EXPERTS, MB_TOK * TOP).astype(jnp.int32)
        ranking = jax.vmap(ranking_of)(blocks)
        slot_table = jnp.full((EXPERTS, EXPERTS, CAP), TOKENS, jnp.int32).at[blocks, sources, ranking].set(token_ids)
        padded = jnp.concatenate([tokens[batch_index], jnp.zeros((1, D), jnp.bfloat16)], axis=0)
        gathered = padded[slot_table.reshape(EXPERTS, EXPERTS * CAP)]
        served = lax.map(serve, (gathered, owner_before.astype(jnp.int32)))
        served = served.reshape(EXPERTS, EXPERTS, CAP, D)
        picked = served[blocks, sources, ranking].reshape(TOKENS, TOP, D).astype(jnp.float32)
        combined = jnp.sum(route_gates[batch_index][:, :, None] * picked, axis=1)
        outputs.append(combined.astype(jnp.bfloat16))
    mixed_tokens = jnp.stack(outputs)
    destination = owner_after[routes]
    matching = destination[..., None] == jnp.arange(EXPERTS, dtype=jnp.int32)
    served_gates = jnp.sum(jnp.where(matching, route_gates[..., None], jnp.float32(0.0)), axis=(0, 1, 2))
    load = EXPERTS * served_gates / jnp.sum(route_gates)
    devices = jnp.arange(EXPERTS, dtype=jnp.int32)
    holding = jnp.where(swap_flags == 1, jnp.bitwise_xor(devices, halfway), devices).astype(jnp.int32)
    held_gate_up = w_gate_up[holding]
    held_down = w_down[holding]
    return mixed_tokens, load, held_gate_up, held_down
```

```python
import jax
import jax.numpy as jnp
from jax import lax
from jax.sharding import PartitionSpec as P


def partner_2(value, axis, stride):
    return lax.ppermute(value, axis, [(i, i ^ 1 << stride) for i in range(lax.axis_size(axis))])


def swiglu(inputs, gate_up, down_weight):
    hidden_width = down_weight.shape[0]
    hidden = jnp.dot(inputs, gate_up, preferred_element_type=jnp.float32)
    activated = (jax.nn.silu(hidden[:, :hidden_width]) * hidden[:, hidden_width:]).astype(
        jnp.bfloat16
    )
    return jnp.dot(activated, down_weight, preferred_element_type=jnp.float32).astype(jnp.bfloat16)


def slot_tables(route_block, gate_block, placement_table, experts, capacity):
    batch_rows, top_count = route_block.shape
    flattened = route_block.reshape(-1)
    onehot = flattened[:, None] == jnp.arange(experts, dtype=jnp.int32)[None, :]
    places = jnp.arange(batch_rows * top_count, dtype=jnp.int32)
    same = flattened[:, None] == flattened[None, :]
    ranking = jnp.sum((same & (places[None, :] < places[:, None])).astype(jnp.int32), axis=1)
    placed = jnp.sum(jnp.where(onehot, placement_table[None, :], 0), axis=1)
    slot_ids = placed * capacity + ranking
    matches = slot_ids[:, None] == jnp.arange(experts * capacity, dtype=jnp.int32)[None, :]
    placing = jnp.any(matches.reshape(batch_rows, top_count, -1), axis=1).astype(jnp.bfloat16)
    weighting = jnp.sum(
        jnp.where(matches, gate_block.reshape(-1)[:, None], jnp.float32(0.0)).reshape(
            batch_rows, top_count, -1
        ),
        axis=1,
    )
    return (placing, weighting)


def shards(tokens, routes, route_gates, w_gate_up, w_down, owner_before, swap_flags):
    experts = lax.axis_size("expert")
    device = lax.axis_index("expert")
    halfway = experts // 2
    batches, batch_rows, model_width = tokens.shape
    top_count = routes.shape[2]
    capacity = max(2, (2 * batch_rows * top_count + experts - 1) // experts)
    swapped = swap_flags[owner_before] == 1
    owner_after = jnp.where(swapped, jnp.bitwise_xor(owner_before, halfway), owner_before)
    far_bit = experts.bit_length() - 2
    own_weights = (w_gate_up[0], w_down[0])
    partner = partner_2((w_gate_up[0], w_down[0]), "expert", far_bit)
    moving = swap_flags[device] == 1
    new_weights = lax.cond(moving, lambda: partner, lambda: own_weights)

    placing, weighting = jax.vmap(
        lambda r, g: slot_tables(r, g, owner_before, experts, capacity)
    )(routes, route_gates)
    filled = jnp.einsum("mts,mtd->msd", placing, tokens, preferred_element_type=jnp.float32)
    filled = filled.astype(jnp.bfloat16).reshape(batches, experts, capacity, model_width)
    filled = filled.transpose(1, 0, 2, 3).reshape(experts, batches * capacity, model_width)
    received = lax.all_to_all(filled, "expert", split_axis=0, concat_axis=0, tiled=True)
    results = swiglu(received.reshape(-1, model_width), w_gate_up[0], w_down[0]).reshape(
        experts, batches * capacity, model_width
    )
    returned = lax.all_to_all(results, "expert", split_axis=0, concat_axis=0, tiled=True)
    returned = returned.reshape(experts, batches, capacity, model_width).transpose(1, 0, 2, 3)
    returned = returned.reshape(batches, experts * capacity, model_width)
    mixed_tokens = jnp.einsum(
        "mts,msd->mtd",
        weighting,
        returned.astype(jnp.float32),
        precision=lax.Precision.HIGHEST,
    ).astype(jnp.bfloat16)
    destination = owner_after[routes]
    matching = destination[..., None] == jnp.arange(experts, dtype=jnp.int32)
    dest_gates = jnp.sum(
        jnp.where(matching, route_gates[..., None], jnp.float32(0.0)), axis=(0, 1, 2)
    )
    served = lax.psum_scatter(dest_gates, "expert", scatter_dimension=0, tiled=True)
    total = lax.psum(jnp.sum(route_gates), "expert")
    load = experts * served / total
    return (mixed_tokens, load, new_weights[0][None], new_weights[1][None])


def solution(mesh):
    return jax.shard_map(
        shards,
        mesh=mesh,
        in_specs=(
            P(None, ("dp", "expert"), None),
            P(None, ("dp", "expert"), None),
            P(None, ("dp", "expert"), None),
            P("expert", None, None),
            P("expert", None, None),
            P(),
            P(),
        ),
        out_specs=(
            P(None, ("dp", "expert"), None),
            P(("dp", "expert")),
            P(("dp", "expert"), None, None),
            P(("dp", "expert"), None, None),
        ),
        check_vma=False,
    )
```

```python
import functools

import jax
import jax.numpy as jnp
from jax import lax
from jax.experimental import pallas as pl
from jax.experimental.pallas import tpu as pltpu
from jax.sharding import PartitionSpec as P

MESH = pl.DeviceIdType.MESH
MB, T, D, F = 4, 16, 2048, 768
CAP = 4
NQ = 8
ND = 8
ROWS = NQ * CAP
LANES = NQ * T
GCH, DCH = 8, 4
GROWS, DROWS = 1024 // GCH, 384 // DCH
NW = GCH + DCH


def layer_kernel(
    tok_ref, meta_ref, wgu_hbm, wd_hbm,
    out_ref, stat_ref, ngu_hbm, nd_hbm,
    wgu, wd, xp, mp, slot_t, gate_t, p2s, r2, act, y, r3, p4s, r4, st_s, st_r, pv_s, pv_r,
    load_sem, p1_s, p1_r, m_s, m_r, p2_ss, p2_r, t_s, t_r, p3_s, p3_r, p4_ss, p4_r,
    v_s, v_r, wz_s, wz_r, wf_s, wf_r,
):
    e, dp = lax.axis_index("expert"), lax.axis_index("dp")
    z, x, yh, c = e // 16, (e // 4) % 4, (e // 2) % 2, e % 2
    q, d = z * 2 + yh, x * 2 + c

    def plane(i):
        return (i // 2) * 16 + x * 4 + (i % 2) * 2 + c

    def column(i):
        return z * 16 + (i // 2) * 4 + yh * 2 + i % 2

    peers_q = [lax.rem(q + k, NQ) for k in range(1, NQ)]
    peers_d = [lax.rem(d + k, ND) for k in range(1, ND)]
    partner = lax.rem(e + 32, 64)

    def remote(src, dst, s, r, dev, other=None):
        return pltpu.make_async_remote_copy(
            src_ref=src, dst_ref=dst, send_sem=s, recv_sem=r,
            device_id=(dev, dp if other is None else other), device_id_type=MESH,
        )

    load_gu = pltpu.make_async_copy(wgu_hbm, wgu, load_sem.at[0])
    load_d = pltpu.make_async_copy(wd_hbm, wd, load_sem.at[1])
    load_gu.start()
    load_d.start()

    barrier = pltpu.get_barrier_semaphore()
    for i in peers_q:
        pl.semaphore_signal(barrier, inc=1, device_id=(plane(i), dp), device_id_type=MESH)
    for i in peers_d:
        pl.semaphore_signal(barrier, inc=1, device_id=(column(i), dp), device_id_type=MESH)
    pl.semaphore_signal(barrier, inc=1, device_id=(e, 1 - dp), device_id_type=MESH)
    pl.semaphore_wait(barrier, 15)

    def meta_copy(k):
        return remote(meta_ref.at[peers_q[k]], mp.at[q], m_s.at[k], m_r.at[k], plane(peers_q[k]))

    def p1(g, k):
        return remote(tok_ref.at[pl.ds(g * T, T)], xp.at[g, q], p1_s.at[g, k], p1_r.at[g, k], plane(peers_q[k]))

    def p2(g, k):
        return remote(p2s.at[g, peers_d[k]], r2.at[g, d], p2_ss.at[g, k], p2_r.at[g, k], column(peers_d[k]))

    def stat(k):
        return remote(st_s, st_r.at[d], t_s.at[k], t_r.at[k], column(peers_d[k]))

    def p3(g, k):
        return remote(y.at[g, peers_d[k]], r3.at[g, d], p3_s.at[g, k], p3_r.at[g, k], column(peers_d[k]))

    def p4(g, k):
        return remote(p4s.at[g, peers_q[k]], r4.at[g, q], p4_ss.at[g, k], p4_r.at[g, k], plane(peers_q[k]))

    def weight_rows(i):
        if i < GCH:
            rows = pl.ds(pl.multiple_of(dp * 1024 + i * GROWS, 16), GROWS)
            return wgu_hbm.at[rows], ngu_hbm.at[rows]
        rows = pl.ds(pl.multiple_of(dp * 384 + (i - GCH) * DROWS, 16), DROWS)
        return wd_hbm.at[rows], nd_hbm.at[rows]

    def w_z(i):
        src, dst = weight_rows(i)
        return remote(src, dst, wz_s.at[i], wz_r.at[i], partner)

    def w_f(i):
        _, dst = weight_rows(i)
        return remote(dst, dst, wf_s.at[i], wf_r.at[i], e, 1 - dp)

    def forward(i):
        w_z(i).wait_recv()
        w_f(i).start()

    for k in range(7):
        meta_copy(k).start()
    for g in range(MB):
        for k in range(7):
            p1(g, k).start()
    for i in range(NW):
        w_z(i).start()

    mp[q] = meta_ref[q]
    for g in range(MB):
        xp[g, q] = tok_ref[pl.ds(g * T, T), :]
    for k in range(7):
        meta_copy(k).wait_recv()

    lane = lax.broadcasted_iota(jnp.int32, (16, 128), 1)
    totals = jnp.zeros((8, 128), jnp.float32)
    for b in range(NQ):
        totals = totals + mp[b, 16:24, :]
    served = jnp.zeros((8, 128), jnp.float32)
    for g in range(MB):
        both = jnp.zeros((16, 128), jnp.float32)
        for b in range(NQ):
            turned = pltpu.roll(mp[b, 0:16, :], (b * T - g * T) % 128, 1)
            both = jnp.where(lane // T == b, turned, both)
        slot_t[g] = both[0:8]
        gate_t[g] = both[8:16]
        served = served + both[8:16]
    st_s[0:8, :] = served
    st_s[8:16, :] = totals
    for k in range(7):
        stat(k).start()
    st_r[d] = st_s[...]

    block = lax.broadcasted_iota(jnp.int32, (ROWS, LANES), 0)
    spot = (block % CAP + 1).astype(jnp.float32)
    same = block // CAP == lax.broadcasted_iota(jnp.int32, (ROWS, LANES), 1) // T

    def picks(g, j):
        return same & (jnp.broadcast_to(slot_t[g, pl.ds(j, 1), :], (ROWS, LANES)) == spot)

    for g in range(MB):
        for k in range(7):
            p1(g, k).wait_recv()
        rows_in = xp[g].reshape(LANES, D)
        chosen = jnp.concatenate(
            [jnp.where(picks(g, j), 1.0, 0.0).astype(jnp.bfloat16) for j in range(ND)], axis=0
        )
        for t in range(4):
            cols = pl.ds(t * 512, 512)
            part = jnp.dot(chosen, rows_in[:, t * 512:(t + 1) * 512], preferred_element_type=jnp.float32)
            p2s[g, :, :, cols] = part.astype(jnp.bfloat16).reshape(ND, ROWS, 512)
        for k in range(7):
            p2(g, k).start()
        r2[g, d] = p2s[g, d]

    load_gu.wait()
    load_d.wait()

    for g in range(MB):
        for k in range(7):
            p2(g, k).wait_recv()

        @pl.loop(0, F // 256)
        def _(t):
            rows_in = r2[g].reshape(ND * ROWS, D)
            at = pl.multiple_of(t * 256, 256)
            up_at = pl.multiple_of(F + t * 256, 256)
            gate = jnp.dot(rows_in, wgu[:, pl.ds(at, 256)], preferred_element_type=jnp.float32)
            up = jnp.dot(rows_in, wgu[:, pl.ds(up_at, 256)], preferred_element_type=jnp.float32)
            act[:, pl.ds(at, 256)] = (gate / (1.0 + jnp.exp(-gate)) * up).astype(jnp.bfloat16)

        @pl.loop(0, D // 512)
        def _(t):
            cols = pl.ds(pl.multiple_of(t * 512, 512), 512)
            part = jnp.dot(act[...], wd[:, cols], preferred_element_type=jnp.float32)
            y[g, :, :, cols] = part.astype(jnp.bfloat16).reshape(ND, ROWS, 512)

        for k in range(7):
            p3(g, k).start()
        r3[g, d] = y[g, d]
        forward(g)

    for k in range(7):
        stat(k).wait_recv()
    mine = jnp.zeros((1, 128), jnp.float32)
    whole = jnp.zeros((8, 128), jnp.float32)
    for s in range(ND):
        mine = mine + st_r[s, pl.ds(d, 1), :]
        whole = whole + st_r[s, 8:16, :]
    mine = jnp.broadcast_to(jnp.sum(mine, axis=1, keepdims=True), (8, 128))
    whole = jnp.broadcast_to(jnp.sum(jnp.sum(whole, axis=0, keepdims=True), axis=1, keepdims=True), (8, 128))
    pv_s[...] = mine
    swap_load = remote(pv_s, pv_r, v_s, v_r, partner)
    swap_load.start()

    for g in range(MB):
        for k in range(7):
            p3(g, k).wait_recv()
        weights = jnp.concatenate(
            [
                jnp.where(picks(g, j), jnp.broadcast_to(gate_t[g, pl.ds(j, 1), :], (ROWS, LANES)), 0.0)
                for j in range(ND)
            ],
            axis=0,
        ).T
        high = weights.astype(jnp.bfloat16)
        low = (weights - high.astype(jnp.float32)).astype(jnp.bfloat16)
        rows_back = r3[g].reshape(ND * ROWS, D)
        for t in range(4):
            cols = pl.ds(t * 512, 512)
            back = rows_back[:, t * 512:(t + 1) * 512]
            part = jnp.dot(high, back, preferred_element_type=jnp.float32)
            part = part + jnp.dot(low, back, preferred_element_type=jnp.float32)
            p4s[g, :, :, cols] = part.astype(jnp.bfloat16).reshape(NQ, T, 512)
        for k in range(7):
            p4(g, k).start()
        r4[g, q] = p4s[g, q]
        forward(MB + g)
    for i in range(2 * MB, NW):
        forward(i)

    swap_load.wait()
    stat_ref[0:8, :] = mine
    stat_ref[8:16, :] = pv_r[...]
    stat_ref[16:24, :] = whole

    for g in range(MB):
        for k in range(7):
            p4(g, k).wait_recv()
        total = r4[g, 0].astype(jnp.float32)
        for b in range(1, NQ):
            total = total + r4[g, b].astype(jnp.float32)
        out_ref[pl.ds(g * T, T), :] = total.astype(jnp.bfloat16)

    for i in range(NW):
        w_z(i).wait_send()
        w_f(i).wait()
    for k in range(7):
        meta_copy(k).wait_send()
        stat(k).wait_send()
        for g in range(MB):
            p1(g, k).wait_send()
            p2(g, k).wait_send()
            p3(g, k).wait_send()
            p4(g, k).wait_send()


def fused_layer(tok, meta, wgu, wd):
    dma = pltpu.SemaphoreType.DMA
    bf = jnp.bfloat16
    vm = pl.BlockSpec(memory_space=pltpu.VMEM)
    hbm = pl.BlockSpec(memory_space=pl.ANY)
    return pl.pallas_call(
        layer_kernel,
        out_shape=(
            jax.ShapeDtypeStruct((MB * T, D), bf),
            jax.ShapeDtypeStruct((24, 128), jnp.float32),
            jax.ShapeDtypeStruct(wgu.shape, bf),
            jax.ShapeDtypeStruct(wd.shape, bf),
        ),
        in_specs=[vm, vm, hbm, hbm],
        out_specs=(vm, vm, hbm, hbm),
        scratch_shapes=[
            pltpu.VMEM((D, 2 * F), bf),
            pltpu.VMEM((F, D), bf),
            pltpu.VMEM((MB, NQ, T, D), bf),
            pltpu.VMEM((NQ, 24, 128), jnp.float32),
            pltpu.VMEM((MB, 8, 128), jnp.float32),
            pltpu.VMEM((MB, 8, 128), jnp.float32),
            pltpu.VMEM((MB, ND, ROWS, D), bf),
            pltpu.VMEM((MB, ND, ROWS, D), bf),
            pltpu.VMEM((ND * ROWS, F), bf),
            pltpu.VMEM((MB, ND, ROWS, D), bf),
            pltpu.VMEM((MB, ND, ROWS, D), bf),
            pltpu.VMEM((MB, NQ, T, D), bf),
            pltpu.VMEM((MB, NQ, T, D), bf),
            pltpu.VMEM((16, 128), jnp.float32),
            pltpu.VMEM((ND, 16, 128), jnp.float32),
            pltpu.VMEM((8, 128), jnp.float32),
            pltpu.VMEM((8, 128), jnp.float32),
            dma((2,)),
            dma((MB, 7)), dma((MB, 7)),
            dma((7,)), dma((7,)),
            dma((MB, 7)), dma((MB, 7)),
            dma((7,)), dma((7,)),
            dma((MB, 7)), dma((MB, 7)),
            dma((MB, 7)), dma((MB, 7)),
            dma, dma,
            dma((NW,)), dma((NW,)),
            dma((NW,)), dma((NW,)),
        ],
        compiler_params=pltpu.CompilerParams(
            collective_id=0, has_side_effects=True, vmem_limit_bytes=52 * 2**20
        ),
        name="layer",
    )(tok, meta, wgu, wd)


def keep_kernel(flags, gu, dn, ngu, nd, held_gu, held_d, sems):
    moving = flags[lax.axis_index("expert")] == 1
    parts = []
    for i in range(4):
        a, b = pl.ds(i * 512, 512), pl.ds(i * 192, 192)
        parts.append((gu.at[a], ngu.at[a], held_gu.at[a], sems.at[2 * i]))
        parts.append((dn.at[b], nd.at[b], held_d.at[b], sems.at[2 * i + 1]))

    @pl.when(moving)
    def _():
        for _, new, out, sem in parts:
            pltpu.make_async_copy(new, out, sem).start()

    @pl.when(jnp.logical_not(moving))
    def _():
        for own, _, out, sem in parts:
            pltpu.make_async_copy(own, out, sem).start()

    for own, _, out, sem in parts:
        pltpu.make_async_copy(own, out, sem).wait()


def keep(flags, gu, dn, ngu, nd):
    hbm = pl.BlockSpec(memory_space=pl.ANY)
    return pl.pallas_call(
        keep_kernel,
        out_shape=(jax.ShapeDtypeStruct(gu.shape, gu.dtype), jax.ShapeDtypeStruct(dn.shape, dn.dtype)),
        in_specs=[pl.BlockSpec(memory_space=pltpu.SMEM), hbm, hbm, hbm, hbm],
        out_specs=(hbm, hbm),
        scratch_shapes=[pltpu.SemaphoreType.DMA((8,))],
        name="keep",
    )(flags, gu, dn, ngu, nd)


def route_tables(routes, gates, owner_before):
    experts = owner_before.shape[0]
    ids = jnp.arange(experts, dtype=jnp.int32)
    held = jnp.sum(jnp.where(owner_before[None, :] == ids[:, None], ids[None, :], 0), axis=1)
    r, g = routes.reshape(MB, T, -1), gates.reshape(MB, T, -1)
    match = r[None] == held[:, None, None, None]
    gate = jnp.sum(jnp.where(match, g[None], 0.0), axis=3)
    sent = jnp.any(match, axis=3)
    before = jnp.arange(T)[:, None] < jnp.arange(T)[None, :]
    rank = jnp.sum(jnp.where(before & sent[..., None], 1.0, 0.0), axis=2)
    slot = jnp.where(sent, rank + 1.0, 0.0)

    def by_plane(a):
        a = a.reshape(4, 4, 2, 2, MB * T).transpose(0, 2, 1, 3, 4)
        return a.reshape(NQ, ND, MB * T)

    sums = jnp.sum(g, axis=2).reshape(1, 1, MB * T)
    sums = jnp.pad(jnp.broadcast_to(sums, (NQ, 1, MB * T)), ((0, 0), (0, 7), (0, 0)))
    table = jnp.concatenate([by_plane(slot), by_plane(gate), sums], axis=1)
    return jnp.pad(table, ((0, 0), (0, 0), (0, 128 - MB * T)))


def shards(tokens, routes, route_gates, w_gate_up, w_down, owner_before, swap_flags):
    meta = route_tables(routes, route_gates, owner_before)
    gu, dn = w_gate_up[0], w_down[0]
    mixed, stat, ngu, nd = fused_layer(tokens.reshape(MB * T, D), meta, gu, dn)
    held_gu, held_d = keep(swap_flags, gu, dn, ngu, nd)
    moving = swap_flags[lax.axis_index("expert")] == 1
    served = jnp.where(moving, stat[8:9, 0], stat[0:1, 0])
    load = owner_before.shape[0] * served / stat[16:17, 0]
    return mixed.reshape(MB, T, D), load, held_gu[None], held_d[None]


def solution(mesh):
    return jax.shard_map(
        shards,
        mesh=mesh,
        in_specs=(
            P(None, ("dp", "expert"), None),
            P(None, ("dp", "expert"), None),
            P(None, ("dp", "expert"), None),
            P("expert", None, None),
            P("expert", None, None),
            P(),
            P(),
        ),
        out_specs=(
            P(None, ("dp", "expert"), None),
            P(("dp", "expert")),
            P(("dp", "expert"), None, None),
            P(("dp", "expert"), None, None),
        ),
        check_vma=False,
    )
```

```python
import functools

import jax
import jax.numpy as jnp
from jax import lax
from jax.experimental import pallas as pl
from jax.experimental.pallas import tpu as pltpu
from jax.sharding import PartitionSpec as P

MESH = pl.DeviceIdType.MESH
MB, T, D, F = 4, 16, 2048, 768
CAP = 4
NQ = 8
ND = 8
ROWS = NQ * CAP
LANES = NQ * T
GCH, DCH = 16, 8
GROWS, DROWS = 1024 // GCH, 384 // DCH
NW = GCH + DCH
AHEAD = 3
P1_WAY = (1, 2, 1, 2)
P4_WAY = (1, 2, 1, 2)
ORDER = (
    "go.0", "tables", "go.1", "relay.0", "go.2", "go.3", "meta", "p2.0",
    "relay.1", "relay.2", "relay.3", "p2.1", "p2.2", "p2.3", "send.0-3",
    "ffn.0", "pass.0-3", "ffn.1", "pass.3-6", "ffn.2", "pass.6-8", "ffn.3", "pass.8-11", "load",
    "mix.0", "pass.11-13", "mix.1", "mid.0", "pass.13-15", "mix.2", "mid.1", "pass.15-18", "mix.3", "mid.2", "pass.18-21",
    "end.0", "end.1", "mid.3", "pass.21-24", "end.2", "end.3",
)


def route_tables(routes_ref, gates_ref, owner_ref, meta_ref):
    experts = NQ * ND
    place = lax.broadcasted_iota(jnp.int32, (experts, experts), 0)
    location = (place // 8 % 4) * 16 + (place // 2 % 4) * 4 + (place // 32) * 2 + place % 2
    expert = lax.broadcasted_iota(jnp.int32, (experts, experts), 1)
    here = jnp.broadcast_to(owner_ref[...], (experts, experts)) == location
    held = jnp.sum(jnp.where(here, expert.astype(jnp.float32), 0.0), axis=1, keepdims=True)
    held = jnp.broadcast_to(held, (experts, 128))
    rest = 128 - MB * T
    routes = [routes_ref[g].astype(jnp.float32) for g in range(MB)] + [jnp.full((8, rest), -1.0, jnp.float32)]
    routes = jnp.concatenate(routes, axis=1)
    gates = jnp.concatenate([gates_ref[g] for g in range(MB)] + [jnp.zeros((8, rest), jnp.float32)], axis=1)
    gate = jnp.zeros((experts, 128), jnp.float32)
    sent = jnp.zeros((experts, 128), jnp.float32)
    for k in range(8):
        match = jnp.broadcast_to(routes[k:k + 1], (experts, 128)) == held
        gate = jnp.where(match, jnp.broadcast_to(gates[k:k + 1], (experts, 128)), gate)
        sent = jnp.where(match, 1.0, sent)
    one = lax.broadcasted_iota(jnp.int32, (128, 128), 0)
    two = lax.broadcasted_iota(jnp.int32, (128, 128), 1)
    before = jnp.where((one < two) & (one // T == two // T), 1.0, 0.0).astype(jnp.bfloat16)
    rank = jnp.dot(sent.astype(jnp.bfloat16), before, preferred_element_type=jnp.float32)
    slot = jnp.where(sent > 0.0, rank + 1.0, 0.0)
    for i in range(NQ):
        meta_ref[i, 0:8] = slot[i * 8:(i + 1) * 8]
        meta_ref[i, 8:16] = gate[i * 8:(i + 1) * 8]
        meta_ref[i, 16:24] = gates


def layer_kernel(
    tok_hbm, routes_hbm, gates_hbm, owner_hbm, flags_hbm, wgu_hbm, wd_hbm,
    out_ref, load_ref, ngu, nd,
    wgu, wd, routes_ref, gates_ref, owner_ref, flags_ref, meta_ref, xp, mp, slot_t, gate_t, p2s, r2, act, r3, p4s, rs, ry, rz, st_s, st_r, pv_s, pv_r, whole_ref,
    load_sem, p1_s, p1_r, m_s, m_r, p2_ss, p2_r, t_s, t_r, p3_s, p3_r, p4_ss, p4_r,
    v_s, v_r, wz_s, wz_r, wf_s, wf_r,
):
    e, dp = lax.axis_index("expert"), lax.axis_index("dp")
    z, x, yh, c = e // 16, (e // 4) % 4, (e // 2) % 2, e % 2
    q, d = yh * 4 + z, x * 2 + c
    other_y = 1 - yh

    def plane(i):
        return (i % 4) * 16 + x * 4 + (i // 4) * 2 + c

    def column(i):
        return z * 16 + (i // 2) * 4 + yh * 2 + i % 2

    peers_q = [lax.rem(q + k, NQ) for k in range(1, NQ)]
    peers_d = [lax.rem(d + k, ND) for k in range(1, ND)]
    partner = lax.rem(e + 32, 64)
    peers_z = [lax.rem(z + k, 4) for k in range(1, 4)]
    from_z = [lax.rem(z + 4 - k, 4) for k in range(1, 4)]
    across = plane(other_y * 4 + z)

    def remote(src, dst, s, r, dev, other=None):
        return pltpu.make_async_remote_copy(
            src_ref=src, dst_ref=dst, send_sem=s, recv_sem=r,
            device_id=(dev, dp if other is None else other), device_id_type=MESH,
        )

    small = [
        pltpu.make_async_copy(routes_hbm, routes_ref, load_sem.at[2]),
        pltpu.make_async_copy(gates_hbm, gates_ref, load_sem.at[3]),
        pltpu.make_async_copy(owner_hbm, owner_ref, load_sem.at[4]),
    ]
    small.append(pltpu.make_async_copy(flags_hbm, flags_ref, load_sem.at[5 + MB]))
    small += [pltpu.make_async_copy(tok_hbm.at[g], xp.at[g, q], load_sem.at[5 + g]) for g in range(MB)]
    for copy in small:
        copy.start()
    load_gu = pltpu.make_async_copy(wgu_hbm, wgu, load_sem.at[0])
    load_d = pltpu.make_async_copy(wd_hbm, wd, load_sem.at[1])

    barrier = pltpu.get_barrier_semaphore()
    for i in peers_q:
        pl.semaphore_signal(barrier, inc=1, device_id=(plane(i), dp), device_id_type=MESH)
    for i in peers_d:
        pl.semaphore_signal(barrier, inc=1, device_id=(column(i), dp), device_id_type=MESH)
    pl.semaphore_signal(barrier, inc=1, device_id=(e, 1 - dp), device_id_type=MESH)
    pl.semaphore_wait(barrier, 15)

    def meta_copy(k):
        return remote(meta_ref.at[peers_q[k]], mp.at[q], m_s.at[k], m_r.at[k], plane(peers_q[k]))

    def p1(g, k):
        own = tok_hbm.at[g]
        if k < 3:
            src, dst, to = own, xp.at[g, q], plane(yh * 4 + peers_z[k])
        elif k == 3:
            src, dst, to = own, xp.at[g, q], across
        elif P1_WAY[g] == 0:
            src, dst, to = own, xp.at[g, q], plane(other_y * 4 + peers_z[k - 4])
        elif P1_WAY[g] == 1:
            src = dst = xp.at[g, yh * 4 + from_z[k - 4]]
            to = across
        else:
            src = dst = xp.at[g, other_y * 4 + z]
            to = plane(yh * 4 + peers_z[k - 4])
        return remote(src, dst, p1_s.at[g, k], p1_r.at[g, k], to)

    def p2(g, k):
        return remote(p2s.at[g, peers_d[k]], r2.at[g, d], p2_ss.at[g, k], p2_r.at[g, k], column(peers_d[k]))

    def stat(k):
        return remote(st_s, st_r.at[d], t_s.at[k], t_r.at[k], column(peers_d[k]))

    def p3(g, k):
        return remote(p2s.at[g, peers_d[k]], r3.at[g, d], p3_s.at[g, k], p3_r.at[g, k], column(peers_d[k]))

    def p4_copies(g, hop):
        def along_y(src, dst):
            return remote(src, dst, p4_ss.at[g, 3], p4_r.at[g, 3], across)

        def along_z(src, dst, n, k, y_hi=yh):
            return remote(src, dst, p4_ss.at[g, n], p4_r.at[g, n], plane(y_hi * 4 + peers_z[k]))

        if P4_WAY[g] == 0:
            if hop == 1:
                return []
            copies = [along_z(p4s.at[g, yh * 4 + peers_z[k]], rz.at[g, yh, z], k, k) for k in range(3)]
            copies += [
                along_z(p4s.at[g, other_y * 4 + peers_z[k]], rz.at[g, yh, z], 4 + k, k, other_y) for k in range(3)
            ]
            return copies + [along_y(p4s.at[g, other_y * 4 + z], rz.at[g, yh, z])]
        if P4_WAY[g] == 1:
            if hop == 0:
                return [along_y(p4s.at[g, pl.ds(other_y * 4, 4)], ry.at[g])]
            return [along_z(rs.at[g, peers_z[k]], rz.at[g, 0, z], k, k) for k in range(3)]
        if hop == 0:
            return [
                along_z(p4s.at[g, i * 4 + peers_z[k]], rz.at[g, i, z], 4 * i + k, k)
                for i in range(2) for k in range(3)
            ]
        return [along_y(rs.at[g, other_y], ry.at[g, 0])]

    def sum_z(g, i):
        total = rz[g, i, 0].astype(jnp.float32)
        for s in range(1, 4):
            total = total + rz[g, i, s].astype(jnp.float32)
        return total

    def p4_begin(g):
        for copy in p4_copies(g, 0):
            copy.start()
        if P4_WAY[g] == 0:
            rz[g, yh, z] = p4s[g, q]
        if P4_WAY[g] == 2:
            for i in range(2):
                rz[g, i, z] = p4s[g, i * 4 + z]

    def p4_middle(g):
        for copy in p4_copies(g, 0):
            copy.wait_recv()
        if P4_WAY[g] == 1:
            for i in range(4):
                both = p4s[g, yh * 4 + i].astype(jnp.float32) + ry[g, i].astype(jnp.float32)
                rs[g, i] = both.astype(jnp.bfloat16)
            rz[g, 0, z] = rs[g, z]
        if P4_WAY[g] == 2:
            for i in range(2):
                rs[g, i] = sum_z(g, i).astype(jnp.bfloat16)
        for copy in p4_copies(g, 1):
            copy.start()

    def p4_end(g):
        for copy in p4_copies(g, 1):
            copy.wait_recv()
        if P4_WAY[g] == 0:
            total = sum_z(g, 0) + sum_z(g, 1)
        elif P4_WAY[g] == 1:
            total = sum_z(g, 0)
        else:
            total = sum_z(g, yh) + ry[g, 0].astype(jnp.float32)
        out_ref[pl.ds(g * T, T), :] = total.astype(jnp.bfloat16)

    def weight_rows(i):
        if i < GCH:
            rows = pl.ds(pl.multiple_of(dp * 1024 + i * GROWS, 16), GROWS)
            return wgu_hbm.at[rows], ngu.at[rows]
        rows = pl.ds(pl.multiple_of(dp * 384 + (i - GCH) * DROWS, 16), DROWS)
        return wd_hbm.at[rows], nd.at[rows]

    def w_z(i):
        src, dst = weight_rows(i)
        return remote(src, dst, wz_s.at[i], wz_r.at[i], partner)

    def w_f(i):
        _, dst = weight_rows(i)
        return remote(dst, dst, wf_s.at[i], wf_r.at[i], e, 1 - dp)

    block = lax.broadcasted_iota(jnp.int32, (ROWS, LANES), 0)
    spot = (block % CAP + 1).astype(jnp.float32)
    same = block // CAP == lax.broadcasted_iota(jnp.int32, (ROWS, LANES), 1) // T

    def picks(g, j):
        return same & (jnp.broadcast_to(slot_t[g, pl.ds(j, 1), :], (ROWS, LANES)) == spot)

    def moves():
        own_lane = lax.broadcasted_iota(jnp.int32, flags_ref.shape, 1) == e
        return jnp.sum(jnp.where(own_lane, flags_ref[...].astype(jnp.float32), 0.0), axis=1, keepdims=True)

    def do_go(g):
        for k in range(4 if P1_WAY[g] else 7):
            p1(g, k).start()

    def do_tables():
        for copy in small[:4]:
            copy.wait()
        route_tables(routes_ref, gates_ref, owner_ref, meta_ref)
        for k in range(7):
            meta_copy(k).start()
        load_gu.start()
        load_d.start()
        mp[q] = meta_ref[q]
        for copy in small[4:]:
            copy.wait()

    def do_relay(g):
        for k in range(4):
            p1(g, k).wait_recv()
        if P1_WAY[g]:
            for k in range(4, 7):
                p1(g, k).start()

    def do_meta():
        for k in range(7):
            meta_copy(k).wait_recv()
        lane = lax.broadcasted_iota(jnp.int32, (16, 128), 1)
        totals = jnp.zeros((8, 128), jnp.float32)
        for b in range(NQ):
            totals = totals + mp[b, 16:24, :]
        served = jnp.zeros((8, 128), jnp.float32)
        for g in range(MB):
            both = jnp.zeros((16, 128), jnp.float32)
            for b in range(NQ):
                turned = pltpu.roll(mp[b, 0:16, :], (b * T - g * T) % 128, 1)
                both = jnp.where(lane // T == b, turned, both)
            slot_t[g] = both[0:8]
            gate_t[g] = both[8:16]
            served = served + both[8:16]
        st_s[0:8, :] = served
        st_s[8:16, :] = totals
        for k in range(7):
            stat(k).start()
        st_r[d] = st_s[...]

    def do_p2(g):
        for k in range(4, 7):
            p1(g, k).wait_recv()
        rows_in = xp[g].reshape(LANES, D)
        chosen = jnp.concatenate(
            [jnp.where(picks(g, j), 1.0, 0.0).astype(jnp.bfloat16) for j in range(ND)], axis=0
        )
        for t in range(4):
            cols = pl.ds(t * 512, 512)
            part = jnp.dot(chosen, rows_in[:, t * 512:(t + 1) * 512], preferred_element_type=jnp.float32)
            p2s[g, :, :, cols] = part.astype(jnp.bfloat16).reshape(ND, ROWS, 512)
        for k in range(7):
            p2(g, k).start()
        r2[g, d] = p2s[g, d]

    def do_ffn(g):
        for k in range(7):
            p2(g, k).wait_recv()

        @pl.loop(0, F // 256)
        def _(t):
            rows_in = r2[g].reshape(ND * ROWS, D)
            at = pl.multiple_of(t * 256, 256)
            up_at = pl.multiple_of(F + t * 256, 256)
            gate = jnp.dot(rows_in, wgu[:, pl.ds(at, 256)], preferred_element_type=jnp.float32)
            up = jnp.dot(rows_in, wgu[:, pl.ds(up_at, 256)], preferred_element_type=jnp.float32)
            act[:, pl.ds(at, 256)] = (gate / (1.0 + jnp.exp(-gate)) * up).astype(jnp.bfloat16)

        for k in range(7):
            p2(g, k).wait_send()

        @pl.loop(0, D // 512)
        def _(t):
            cols = pl.ds(pl.multiple_of(t * 512, 512), 512)
            part = jnp.dot(act[...], wd[:, cols], preferred_element_type=jnp.float32)
            p2s[g, :, :, cols] = part.astype(jnp.bfloat16).reshape(ND, ROWS, 512)

        for k in range(7):
            p3(g, k).start()
        r3[g, d] = p2s[g, d]

    def do_load():
        for k in range(7):
            stat(k).wait_recv()
        mine = jnp.zeros((1, 128), jnp.float32)
        whole = jnp.zeros((8, 128), jnp.float32)
        for s in range(ND):
            mine = mine + st_r[s, pl.ds(d, 1), :]
            whole = whole + st_r[s, 8:16, :]
        whole = jnp.sum(jnp.sum(whole, axis=0, keepdims=True), axis=1, keepdims=True)
        pv_s[...] = jnp.broadcast_to(jnp.sum(mine, axis=1, keepdims=True), (8, 128))
        whole_ref[...] = jnp.broadcast_to(whole, (8, 128))
        swap_load.start()

    def do_mix(g):
        for k in range(7):
            p3(g, k).wait_recv()
        weights = jnp.concatenate(
            [
                jnp.where(picks(g, j), jnp.broadcast_to(gate_t[g, pl.ds(j, 1), :], (ROWS, LANES)), 0.0)
                for j in range(ND)
            ],
            axis=0,
        ).T
        high = weights.astype(jnp.bfloat16)
        low = (weights - high.astype(jnp.float32)).astype(jnp.bfloat16)
        rows_back = r3[g].reshape(ND * ROWS, D)
        for t in range(4):
            cols = pl.ds(t * 512, 512)
            back = rows_back[:, t * 512:(t + 1) * 512]
            part = jnp.dot(high, back, preferred_element_type=jnp.float32)
            part = part + jnp.dot(low, back, preferred_element_type=jnp.float32)
            p4s[g, :, :, cols] = part.astype(jnp.bfloat16).reshape(NQ, T, 512)
        p4_begin(g)

    def do(what):
        name, _, at = what.partition(".")
        first, _, end = at.partition("-")
        if name == "send":
            for i in range(int(first), int(end)):
                w_z(i).start()
        elif name == "pass":
            for i in range(int(first), int(end)):
                w_z(i).wait_recv()
                own, new = (wgu, ngu) if i < GCH else (wd, nd)
                count = GROWS if i < GCH else DROWS
                base = dp * 1024 + i * GROWS if i < GCH else dp * 384 + (i - GCH) * DROWS
                rows = pl.ds(pl.multiple_of(base, 16), count)
                moving = jnp.broadcast_to(moves(), (count, new.shape[1])) > 0
                new[rows, :] = jnp.where(moving, new[rows, :], own[rows, :])
                w_f(i).start()
                if i + AHEAD < NW and AHEAD:
                    w_z(i + AHEAD).start()
        else:
            steps[name](*([int(at)] if at else []))

    steps = {
        "go": do_go, "tables": do_tables, "relay": do_relay, "meta": do_meta, "p2": do_p2, "ffn": do_ffn, "load": do_load,
        "mix": do_mix, "mid": p4_middle, "end": p4_end,
    }
    swap_load = remote(pv_s, pv_r, v_s, v_r, partner)

    waited = False
    for what in ORDER:
        if what.startswith("ffn") and not waited:
            load_gu.wait()
            load_d.wait()
            waited = True
        do(what)

    swap_load.wait()
    served = jnp.where(jnp.broadcast_to(moves(), (8, 128)) > 0, pv_r[...], pv_s[...])
    load_ref[...] = flags_ref.shape[1] * served / whole_ref[...]

    for i in range(NW):
        w_z(i).wait_send()
        w_f(i).wait()
    for g in range(MB):
        for copy in p4_copies(g, 0) + p4_copies(g, 1):
            copy.wait_send()
    for k in range(7):
        meta_copy(k).wait_send()
        stat(k).wait_send()
        for g in range(MB):
            p1(g, k).wait_send()
            p3(g, k).wait_send()


def fused_layer(tok, routes, gates, owner, flags, wgu, wd):
    dma = pltpu.SemaphoreType.DMA
    bf = jnp.bfloat16
    vm = pl.BlockSpec(memory_space=pltpu.VMEM)
    hbm = pl.BlockSpec(memory_space=pltpu.HBM)
    return pl.pallas_call(
        layer_kernel,
        out_shape=(
            jax.ShapeDtypeStruct((MB * T, D), bf),
            jax.ShapeDtypeStruct((8, 128), jnp.float32),
            jax.ShapeDtypeStruct(wgu.shape, bf),
            jax.ShapeDtypeStruct(wd.shape, bf),
        ),
        in_specs=[hbm] * 7,
        out_specs=(vm, vm, vm, vm),
        scratch_shapes=[
            pltpu.VMEM((D, 2 * F), bf),
            pltpu.VMEM((F, D), bf),
            pltpu.VMEM(routes.shape, routes.dtype),
            pltpu.VMEM(gates.shape, gates.dtype),
            pltpu.VMEM(owner.shape, owner.dtype),
            pltpu.VMEM(flags.shape, flags.dtype),
            pltpu.VMEM((NQ, 24, 128), jnp.float32),
            pltpu.VMEM((MB, NQ, T, D), bf),
            pltpu.VMEM((NQ, 24, 128), jnp.float32),
            pltpu.VMEM((MB, 8, 128), jnp.float32),
            pltpu.VMEM((MB, 8, 128), jnp.float32),
            pltpu.VMEM((MB, ND, ROWS, D), bf),
            pltpu.VMEM((MB, ND, ROWS, D), bf),
            pltpu.VMEM((ND * ROWS, F), bf),
            pltpu.VMEM((MB, ND, ROWS, D), bf),
            pltpu.VMEM((MB, NQ, T, D), bf),
            pltpu.VMEM((MB, 4, T, D), bf),
            pltpu.VMEM((MB, 4, T, D), bf),
            pltpu.VMEM((MB, 2, 4, T, D), bf),
            pltpu.VMEM((16, 128), jnp.float32),
            pltpu.VMEM((ND, 16, 128), jnp.float32),
            pltpu.VMEM((8, 128), jnp.float32),
            pltpu.VMEM((8, 128), jnp.float32),
            pltpu.VMEM((8, 128), jnp.float32),
            dma((6 + MB,)),
            dma((MB, 7)), dma((MB, 7)),
            dma((7,)), dma((7,)),
            dma((MB, 7)), dma((MB, 7)),
            dma((7,)), dma((7,)),
            dma((MB, 7)), dma((MB, 7)),
            dma((MB, 8)), dma((MB, 8)),
            dma, dma,
            dma((NW,)), dma((NW,)),
            dma((NW,)), dma((NW,)),
        ],
        compiler_params=pltpu.CompilerParams(
            collective_id=0, has_side_effects=True, vmem_limit_bytes=41 * 2**20
        ),
        name="layer",
    )(tok, routes, gates, owner, flags, wgu, wd)


def shards(tokens, routes, route_gates, w_gate_up, w_down, owner_before, swap_flags):
    by_token = (0, 2, 1)
    mixed, load, held_gu, held_d = fused_layer(
        tokens, routes.transpose(by_token), route_gates.transpose(by_token),
        owner_before.reshape(1, -1), swap_flags.reshape(1, -1), w_gate_up[0], w_down[0],
    )
    return mixed.reshape(MB, T, D), load[0, :1], held_gu[None], held_d[None]


def solution(mesh):
    return jax.shard_map(
        shards,
        mesh=mesh,
        in_specs=(
            P(None, ("dp", "expert"), None),
            P(None, ("dp", "expert"), None),
            P(None, ("dp", "expert"), None),
            P("expert", None, None),
            P("expert", None, None),
            P(),
            P(),
        ),
        out_specs=(
            P(None, ("dp", "expert"), None),
            P(("dp", "expert")),
            P(("dp", "expert"), None, None),
            P(("dp", "expert"), None, None),
        ),
        check_vma=False,
    )
```

```python
import functools

import jax
import jax.numpy as jnp
from jax import lax
from jax.experimental import pallas as pl
from jax.experimental.pallas import tpu as pltpu
from jax.sharding import PartitionSpec as P

MESH = pl.DeviceIdType.MESH
MB, T, D, F = 4, 16, 2048, 768
CAP = 4
NQ = 8
ND = 8
ROWS = NQ * CAP
LANES = NQ * T
GCH, DCH = 16, 8
GROWS, DROWS = 1024 // GCH, 384 // DCH
NW = GCH + DCH
AHEAD = 4
P1_WAY = (1, 2, 1, 2)
P4_WAY = (1, 2, 1, 2)
ORDER = (
    "go.0", "tables", "go.1", "relay.0", "go.2", "go.3", "meta", "p2.0",
    "relay.1", "relay.2", "relay.3", "p2.1", "p2.2", "p2.3", "send.0-4", "pass.0-1",
    "ffn.0", "pass.1-4", "ffn.1", "pass.4-7", "ffn.2", "pass.7-9", "ffn.3", "pass.9-12", "load",
    "mix.0", "pass.12-14", "mix.1", "mid.0", "pass.14-16", "mix.2", "mid.1", "pass.16-19", "mix.3", "mid.2", "pass.19-22",
    "mid.3", "pass.22-24", "end.0", "end.1", "end.2", "end.3",
)


def route_tables(routes_ref, gates_ref, owner_ref, meta_ref):
    experts = NQ * ND
    place = lax.broadcasted_iota(jnp.int32, (experts, experts), 0)
    location = (place // 8 % 4) * 16 + (place // 2 % 4) * 4 + (place // 32) * 2 + place % 2
    expert = lax.broadcasted_iota(jnp.int32, (experts, experts), 1)
    here = jnp.broadcast_to(owner_ref[...], (experts, experts)) == location
    held = jnp.sum(jnp.where(here, expert.astype(jnp.float32), 0.0), axis=1, keepdims=True)
    held = jnp.broadcast_to(held, (experts, 128))
    rest = 128 - MB * T
    routes = [routes_ref[g].astype(jnp.float32) for g in range(MB)] + [jnp.full((8, rest), -1.0, jnp.float32)]
    routes = jnp.concatenate(routes, axis=1)
    gates = jnp.concatenate([gates_ref[g] for g in range(MB)] + [jnp.zeros((8, rest), jnp.float32)], axis=1)
    gate = jnp.zeros((experts, 128), jnp.float32)
    sent = jnp.zeros((experts, 128), jnp.float32)
    for k in range(8):
        match = jnp.broadcast_to(routes[k:k + 1], (experts, 128)) == held
        gate = jnp.where(match, jnp.broadcast_to(gates[k:k + 1], (experts, 128)), gate)
        sent = jnp.where(match, 1.0, sent)
    one = lax.broadcasted_iota(jnp.int32, (128, 128), 0)
    two = lax.broadcasted_iota(jnp.int32, (128, 128), 1)
    before = jnp.where((one < two) & (one // T == two // T), 1.0, 0.0).astype(jnp.bfloat16)
    rank = jnp.dot(sent.astype(jnp.bfloat16), before, preferred_element_type=jnp.float32)
    slot = jnp.where(sent > 0.0, rank + 1.0, 0.0)
    for i in range(NQ):
        meta_ref[i, 0:8] = slot[i * 8:(i + 1) * 8]
        meta_ref[i, 8:16] = gate[i * 8:(i + 1) * 8]
        meta_ref[i, 16:24] = gates


def layer_kernel(
    tok_hbm, routes_hbm, gates_hbm, owner_hbm, flags_hbm, wgu_hbm, wd_hbm,
    out_ref, load_ref, ngu, nd,
    wgu, wd, routes_ref, gates_ref, owner_ref, flags_ref, meta_ref, xp, mp, slot_t, gate_t, p2s, r2, act, r3, p4s, rs, ry, rz, st_s, st_r, pv_s, pv_r, whole_ref,
    load_sem, p1_s, p1_r, m_s, m_r, p2_ss, p2_r, t_s, t_r, p3_s, p3_r, p4_ss, p4_r,
    v_s, v_r, wz_s, wz_r, wf_s, wf_r,
):
    e, dp = lax.axis_index("expert"), lax.axis_index("dp")
    z, x, yh, c = e // 16, (e // 4) % 4, (e // 2) % 2, e % 2
    q, d = yh * 4 + z, x * 2 + c
    other_y = 1 - yh

    def plane(i):
        return (i % 4) * 16 + x * 4 + (i // 4) * 2 + c

    def column(i):
        return z * 16 + (i // 2) * 4 + yh * 2 + i % 2

    peers_q = [lax.rem(q + k, NQ) for k in range(1, NQ)]
    peers_d = [lax.rem(d + k, ND) for k in range(1, ND)]
    partner = lax.rem(e + 32, 64)
    peers_z = [lax.rem(z + k, 4) for k in range(1, 4)]
    from_z = [lax.rem(z + 4 - k, 4) for k in range(1, 4)]
    across = plane(other_y * 4 + z)

    def remote(src, dst, s, r, dev, other=None):
        return pltpu.make_async_remote_copy(
            src_ref=src, dst_ref=dst, send_sem=s, recv_sem=r,
            device_id=(dev, dp if other is None else other), device_id_type=MESH,
        )

    small = [
        pltpu.make_async_copy(routes_hbm, routes_ref, load_sem.at[2]),
        pltpu.make_async_copy(gates_hbm, gates_ref, load_sem.at[3]),
        pltpu.make_async_copy(owner_hbm, owner_ref, load_sem.at[4]),
    ]
    small.append(pltpu.make_async_copy(flags_hbm, flags_ref, load_sem.at[5 + MB]))
    small += [pltpu.make_async_copy(tok_hbm.at[g], xp.at[g, q], load_sem.at[5 + g]) for g in range(MB)]
    for copy in small:
        copy.start()
    load_gu = pltpu.make_async_copy(wgu_hbm, wgu, load_sem.at[0])
    load_d = pltpu.make_async_copy(wd_hbm, wd, load_sem.at[1])

    barrier = pltpu.get_barrier_semaphore()
    for i in peers_q:
        pl.semaphore_signal(barrier, inc=1, device_id=(plane(i), dp), device_id_type=MESH)
    for i in peers_d:
        pl.semaphore_signal(barrier, inc=1, device_id=(column(i), dp), device_id_type=MESH)
    pl.semaphore_signal(barrier, inc=1, device_id=(e, 1 - dp), device_id_type=MESH)
    pl.semaphore_wait(barrier, 15)

    def meta_copy(k):
        return remote(meta_ref.at[peers_q[k]], mp.at[q], m_s.at[k], m_r.at[k], plane(peers_q[k]))

    def p1(g, k):
        own = tok_hbm.at[g]
        if k < 3:
            src, dst, to = own, xp.at[g, q], plane(yh * 4 + peers_z[k])
        elif k == 3:
            src, dst, to = own, xp.at[g, q], across
        elif P1_WAY[g] == 0:
            src, dst, to = own, xp.at[g, q], plane(other_y * 4 + peers_z[k - 4])
        elif P1_WAY[g] == 1:
            src = dst = xp.at[g, yh * 4 + from_z[k - 4]]
            to = across
        else:
            src = dst = xp.at[g, other_y * 4 + z]
            to = plane(yh * 4 + peers_z[k - 4])
        return remote(src, dst, p1_s.at[g, k], p1_r.at[g, k], to)

    def p2(g, k):
        return remote(p2s.at[g, peers_d[k]], r2.at[g, d], p2_ss.at[g, k], p2_r.at[g, k], column(peers_d[k]))

    def stat(k):
        return remote(st_s, st_r.at[d], t_s.at[k], t_r.at[k], column(peers_d[k]))

    def p3(g, k):
        return remote(p2s.at[g, peers_d[k]], r3.at[g, d], p3_s.at[g, k], p3_r.at[g, k], column(peers_d[k]))

    def p4_copies(g, hop):
        def along_y(src, dst):
            return remote(src, dst, p4_ss.at[g, 3], p4_r.at[g, 3], across)

        def along_z(src, dst, n, k, y_hi=yh):
            return remote(src, dst, p4_ss.at[g, n], p4_r.at[g, n], plane(y_hi * 4 + peers_z[k]))

        if P4_WAY[g] == 0:
            if hop == 1:
                return []
            copies = [along_z(p4s.at[g, yh * 4 + peers_z[k]], rz.at[g, yh, z], k, k) for k in range(3)]
            copies += [
                along_z(p4s.at[g, other_y * 4 + peers_z[k]], rz.at[g, yh, z], 4 + k, k, other_y) for k in range(3)
            ]
            return copies + [along_y(p4s.at[g, other_y * 4 + z], rz.at[g, yh, z])]
        if P4_WAY[g] == 1:
            if hop == 0:
                return [along_y(p4s.at[g, pl.ds(other_y * 4, 4)], ry.at[g])]
            return [along_z(rs.at[g, peers_z[k]], rz.at[g, 0, z], k, k) for k in range(3)]
        if hop == 0:
            return [
                along_z(p4s.at[g, i * 4 + peers_z[k]], rz.at[g, i, z], 4 * i + k, k)
                for i in range(2) for k in range(3)
            ]
        return [along_y(rs.at[g, other_y], ry.at[g, 0])]

    def sum_z(g, i):
        total = rz[g, i, 0].astype(jnp.float32)
        for s in range(1, 4):
            total = total + rz[g, i, s].astype(jnp.float32)
        return total

    def p4_begin(g):
        for copy in p4_copies(g, 0):
            copy.start()
        if P4_WAY[g] == 0:
            rz[g, yh, z] = p4s[g, q]
        if P4_WAY[g] == 2:
            for i in range(2):
                rz[g, i, z] = p4s[g, i * 4 + z]

    def p4_middle(g):
        for copy in p4_copies(g, 0):
            copy.wait_recv()
        if P4_WAY[g] == 1:
            for i in range(4):
                both = p4s[g, yh * 4 + i].astype(jnp.float32) + ry[g, i].astype(jnp.float32)
                rs[g, i] = both.astype(jnp.bfloat16)
            rz[g, 0, z] = rs[g, z]
        if P4_WAY[g] == 2:
            for i in range(2):
                rs[g, i] = sum_z(g, i).astype(jnp.bfloat16)
        for copy in p4_copies(g, 1):
            copy.start()

    def p4_end(g):
        for copy in p4_copies(g, 1):
            copy.wait_recv()
        if P4_WAY[g] == 0:
            total = sum_z(g, 0) + sum_z(g, 1)
        elif P4_WAY[g] == 1:
            total = sum_z(g, 0)
        else:
            total = sum_z(g, yh) + ry[g, 0].astype(jnp.float32)
        out_ref[pl.ds(g * T, T), :] = total.astype(jnp.bfloat16)

    def weight_rows(i):
        if i < GCH:
            rows = pl.ds(pl.multiple_of(dp * 1024 + i * GROWS, 16), GROWS)
            return wgu_hbm.at[rows], ngu.at[rows]
        rows = pl.ds(pl.multiple_of(dp * 384 + (i - GCH) * DROWS, 16), DROWS)
        return wd_hbm.at[rows], nd.at[rows]

    def w_z(i):
        src, dst = weight_rows(i)
        return remote(src, dst, wz_s.at[i], wz_r.at[i], partner)

    def w_f(i):
        _, dst = weight_rows(i)
        return remote(dst, dst, wf_s.at[i], wf_r.at[i], e, 1 - dp)

    block = lax.broadcasted_iota(jnp.int32, (ROWS, LANES), 0)
    spot = (block % CAP + 1).astype(jnp.float32)
    same = block // CAP == lax.broadcasted_iota(jnp.int32, (ROWS, LANES), 1) // T

    def picks(g, j):
        return same & (jnp.broadcast_to(slot_t[g, pl.ds(j, 1), :], (ROWS, LANES)) == spot)

    def moves():
        own_lane = lax.broadcasted_iota(jnp.int32, flags_ref.shape, 1) == e
        return jnp.sum(jnp.where(own_lane, flags_ref[...].astype(jnp.float32), 0.0), axis=1, keepdims=True)

    def do_go(g):
        for k in range(4 if P1_WAY[g] else 7):
            p1(g, k).start()

    def do_tables():
        for copy in small[:4]:
            copy.wait()
        route_tables(routes_ref, gates_ref, owner_ref, meta_ref)
        for k in range(7):
            meta_copy(k).start()
        load_gu.start()
        load_d.start()
        mp[q] = meta_ref[q]
        for copy in small[4:]:
            copy.wait()

    def do_relay(g):
        for k in range(4):
            p1(g, k).wait_recv()
        if P1_WAY[g]:
            for k in range(4, 7):
                p1(g, k).start()

    def do_meta():
        for k in range(7):
            meta_copy(k).wait_recv()
        lane = lax.broadcasted_iota(jnp.int32, (16, 128), 1)
        totals = jnp.zeros((8, 128), jnp.float32)
        for b in range(NQ):
            totals = totals + mp[b, 16:24, :]
        served = jnp.zeros((8, 128), jnp.float32)
        for g in range(MB):
            both = jnp.zeros((16, 128), jnp.float32)
            for b in range(NQ):
                turned = pltpu.roll(mp[b, 0:16, :], (b * T - g * T) % 128, 1)
                both = jnp.where(lane // T == b, turned, both)
            slot_t[g] = both[0:8]
            gate_t[g] = both[8:16]
            served = served + both[8:16]
        st_s[0:8, :] = served
        st_s[8:16, :] = totals
        for k in range(7):
            stat(k).start()
        st_r[d] = st_s[...]

    def do_p2(g):
        for k in range(4, 7):
            p1(g, k).wait_recv()
        rows_in = xp[g].reshape(LANES, D)
        chosen = jnp.concatenate(
            [jnp.where(picks(g, j), 1.0, 0.0).astype(jnp.bfloat16) for j in range(ND)], axis=0
        )
        for t in range(4):
            cols = pl.ds(t * 512, 512)
            part = jnp.dot(chosen, rows_in[:, t * 512:(t + 1) * 512], preferred_element_type=jnp.float32)
            p2s[g, :, :, cols] = part.astype(jnp.bfloat16).reshape(ND, ROWS, 512)
        for k in range(7):
            p2(g, k).start()
        r2[g, d] = p2s[g, d]

    def do_ffn(g):
        for k in range(7):
            p2(g, k).wait_recv()

        @pl.loop(0, F // 256)
        def _(t):
            rows_in = r2[g].reshape(ND * ROWS, D)
            at = pl.multiple_of(t * 256, 256)
            up_at = pl.multiple_of(F + t * 256, 256)
            gate = jnp.dot(rows_in, wgu[:, pl.ds(at, 256)], preferred_element_type=jnp.float32)
            up = jnp.dot(rows_in, wgu[:, pl.ds(up_at, 256)], preferred_element_type=jnp.float32)
            act[:, pl.ds(at, 256)] = (gate / (1.0 + jnp.exp(-gate)) * up).astype(jnp.bfloat16)

        for k in range(7):
            p2(g, k).wait_send()

        @pl.loop(0, D // 512)
        def _(t):
            cols = pl.ds(pl.multiple_of(t * 512, 512), 512)
            part = jnp.dot(act[...], wd[:, cols], preferred_element_type=jnp.float32)
            p2s[g, :, :, cols] = part.astype(jnp.bfloat16).reshape(ND, ROWS, 512)

        for k in range(7):
            p3(g, k).start()
        r3[g, d] = p2s[g, d]

    def do_load():
        for k in range(7):
            stat(k).wait_recv()
        mine = jnp.zeros((1, 128), jnp.float32)
        whole = jnp.zeros((8, 128), jnp.float32)
        for s in range(ND):
            mine = mine + st_r[s, pl.ds(d, 1), :]
            whole = whole + st_r[s, 8:16, :]
        whole = jnp.sum(jnp.sum(whole, axis=0, keepdims=True), axis=1, keepdims=True)
        pv_s[...] = jnp.broadcast_to(jnp.sum(mine, axis=1, keepdims=True), (8, 128))
        whole_ref[...] = jnp.broadcast_to(whole, (8, 128))
        swap_load.start()

    def do_mix(g):
        for k in range(7):
            p3(g, k).wait_recv()
        weights = jnp.concatenate(
            [
                jnp.where(picks(g, j), jnp.broadcast_to(gate_t[g, pl.ds(j, 1), :], (ROWS, LANES)), 0.0)
                for j in range(ND)
            ],
            axis=0,
        ).T
        high = weights.astype(jnp.bfloat16)
        low = (weights - high.astype(jnp.float32)).astype(jnp.bfloat16)
        rows_back = r3[g].reshape(ND * ROWS, D)
        for t in range(4):
            cols = pl.ds(t * 512, 512)
            back = rows_back[:, t * 512:(t + 1) * 512]
            part = jnp.dot(high, back, preferred_element_type=jnp.float32)
            part = part + jnp.dot(low, back, preferred_element_type=jnp.float32)
            p4s[g, :, :, cols] = part.astype(jnp.bfloat16).reshape(NQ, T, 512)
        p4_begin(g)

    def do(what):
        name, _, at = what.partition(".")
        first, _, end = at.partition("-")
        if name == "send":
            for i in range(int(first), int(end)):
                w_z(i).start()
        elif name == "pass":
            for i in range(int(first), int(end)):
                w_z(i).wait_recv()
                own, new = (wgu, ngu) if i < GCH else (wd, nd)
                count = GROWS if i < GCH else DROWS
                base = dp * 1024 + i * GROWS if i < GCH else dp * 384 + (i - GCH) * DROWS
                rows = pl.ds(pl.multiple_of(base, 16), count)
                moving = jnp.broadcast_to(moves(), (count, new.shape[1])) > 0
                new[rows, :] = jnp.where(moving, new[rows, :], own[rows, :])
                w_f(i).start()
                if i + AHEAD < NW and AHEAD:
                    w_z(i + AHEAD).start()
        else:
            steps[name](*([int(at)] if at else []))

    steps = {
        "go": do_go, "tables": do_tables, "relay": do_relay, "meta": do_meta, "p2": do_p2, "ffn": do_ffn, "load": do_load,
        "mix": do_mix, "mid": p4_middle, "end": p4_end,
    }
    swap_load = remote(pv_s, pv_r, v_s, v_r, partner)

    waited = False
    for what in ORDER:
        if what.startswith(("ffn", "pass")) and not waited:
            load_gu.wait()
            load_d.wait()
            waited = True
        do(what)

    swap_load.wait()
    served = jnp.where(jnp.broadcast_to(moves(), (8, 128)) > 0, pv_r[...], pv_s[...])
    load_ref[...] = flags_ref.shape[1] * served / whole_ref[...]

    for i in range(NW):
        w_z(i).wait_send()
        w_f(i).wait()
    for g in range(MB):
        for copy in p4_copies(g, 0) + p4_copies(g, 1):
            copy.wait_send()
    for k in range(7):
        meta_copy(k).wait_send()
        stat(k).wait_send()
        for g in range(MB):
            p1(g, k).wait_send()
            p3(g, k).wait_send()


def fused_layer(tok, routes, gates, owner, flags, wgu, wd):
    dma = pltpu.SemaphoreType.DMA
    bf = jnp.bfloat16
    vm = pl.BlockSpec(memory_space=pltpu.VMEM)
    hbm = pl.BlockSpec(memory_space=pltpu.HBM)
    return pl.pallas_call(
        layer_kernel,
        out_shape=(
            jax.ShapeDtypeStruct((MB * T, D), bf),
            jax.ShapeDtypeStruct((8, 128), jnp.float32),
            jax.ShapeDtypeStruct(wgu.shape, bf),
            jax.ShapeDtypeStruct(wd.shape, bf),
        ),
        in_specs=[hbm] * 7,
        out_specs=(vm, vm, vm, vm),
        scratch_shapes=[
            pltpu.VMEM((D, 2 * F), bf),
            pltpu.VMEM((F, D), bf),
            pltpu.VMEM(routes.shape, routes.dtype),
            pltpu.VMEM(gates.shape, gates.dtype),
            pltpu.VMEM(owner.shape, owner.dtype),
            pltpu.VMEM(flags.shape, flags.dtype),
            pltpu.VMEM((NQ, 24, 128), jnp.float32),
            pltpu.VMEM((MB, NQ, T, D), bf),
            pltpu.VMEM((NQ, 24, 128), jnp.float32),
            pltpu.VMEM((MB, 8, 128), jnp.float32),
            pltpu.VMEM((MB, 8, 128), jnp.float32),
            pltpu.VMEM((MB, ND, ROWS, D), bf),
            pltpu.VMEM((MB, ND, ROWS, D), bf),
            pltpu.VMEM((ND * ROWS, F), bf),
            pltpu.VMEM((MB, ND, ROWS, D), bf),
            pltpu.VMEM((MB, NQ, T, D), bf),
            pltpu.VMEM((MB, 4, T, D), bf),
            pltpu.VMEM((MB, 4, T, D), bf),
            pltpu.VMEM((MB, 2, 4, T, D), bf),
            pltpu.VMEM((16, 128), jnp.float32),
            pltpu.VMEM((ND, 16, 128), jnp.float32),
            pltpu.VMEM((8, 128), jnp.float32),
            pltpu.VMEM((8, 128), jnp.float32),
            pltpu.VMEM((8, 128), jnp.float32),
            dma((6 + MB,)),
            dma((MB, 7)), dma((MB, 7)),
            dma((7,)), dma((7,)),
            dma((MB, 7)), dma((MB, 7)),
            dma((7,)), dma((7,)),
            dma((MB, 7)), dma((MB, 7)),
            dma((MB, 8)), dma((MB, 8)),
            dma, dma,
            dma((NW,)), dma((NW,)),
            dma((NW,)), dma((NW,)),
        ],
        compiler_params=pltpu.CompilerParams(
            collective_id=0, has_side_effects=True, vmem_limit_bytes=41 * 2**20
        ),
        name="layer",
    )(*(pltpu.with_memory_space_constraint(a, pltpu.HBM) for a in (tok, routes, gates, owner, flags, wgu, wd)))


def shards(tokens, routes, route_gates, w_gate_up, w_down, owner_before, swap_flags):
    by_token = (0, 2, 1)
    mixed, load, held_gu, held_d = fused_layer(
        tokens, routes.transpose(by_token), route_gates.transpose(by_token),
        owner_before.reshape(1, -1), swap_flags.reshape(1, -1), w_gate_up[0], w_down[0],
    )
    return mixed.reshape(MB, T, D), load[0, :1], held_gu[None], held_d[None]


def solution(mesh):
    return jax.shard_map(
        shards,
        mesh=mesh,
        in_specs=(
            P(None, ("dp", "expert"), None),
            P(None, ("dp", "expert"), None),
            P(None, ("dp", "expert"), None),
            P("expert", None, None),
            P("expert", None, None),
            P(),
            P(),
        ),
        out_specs=(
            P(None, ("dp", "expert"), None),
            P(("dp", "expert")),
            P(("dp", "expert"), None, None),
            P(("dp", "expert"), None, None),
        ),
        check_vma=False,
    )
```
